768 devices in a mesh: dp: 96 (over y_hi, x, z), tensor: 8 (over y_lo, core).
Axes of the slice: x: 4, y: 8 (y_hi: 2, y_lo: 4; y = y_hi * 4 + y_lo), z: 12, core: 2. Of those that a mesh axis runs over, the one named last changes fastest.
Arguments:
- gradient: bfloat16 [96, 2, 128, 14336], P('dp', None, None, 'tensor'), may hold values from -6 to 6
- error_buffer: float32 [96, 2, 128, 14336], P('dp', None, None, 'tensor'), may hold values from -4 to 4
- q_warm: float32 [2, 14336, 64], P(None, 'tensor'), may hold values from -0.046875 to 0.046875
Outputs:
- new_error: float32 [96, 2, 128, 14336], P('dp', None, None, 'tensor')
- p_factor: float32 [2, 128, 64], replicated
- q_factor: float32 [2, 14336, 64], P(None, 'tensor')
The draws below stay inside these ranges and needn't reach their ends.
All inputs are finite; a program needn't handle non-finite values.
Results may differ from the reference program's by a relative error of at most 0.0003.
Values sent between devices are 32-bit elements; how exact they have to be, the bound alone decides.
A program may use at most 32 MiB of HBM per device.

```python
import jax
import jax.numpy as jnp
from jax import lax

FF = 14336
RANK = 64
ROWS = 128
REPLICAS = 96


def level_of(rng, shape, split, smallest, largest):
    def one(dim, parts):
        draws = jax.random.uniform(jax.random.fold_in(jax.random.fold_in(rng, 6), dim), (parts,), jnp.float32, smallest / len(split), largest / len(split))
        return jnp.repeat(jnp.exp(draws), shape[dim] // parts).reshape((-1,) + (1,) * (len(shape) - dim - 1))

    loudness = one(*split[0])
    for cut in split[1:]:
        loudness = loudness * one(*cut)
    return loudness


def centred(rng, dims, spread, reach, split=(), held_as=jnp.bfloat16):
    factor_of = level_of(rng, dims, split, -0.22, 0.18) if split else 1.0
    drawn = jax.random.normal(rng, dims, jnp.float32) * spread * factor_of
    return jnp.minimum(jnp.maximum(drawn, -reach), reach).astype(held_as)


def setup_inputs(seed: int = 0) -> dict:
    keys = jax.random.split(jax.random.key(seed), 4)
    return {
        "gradient": centred(keys[0], (REPLICAS, 2, ROWS, FF), 1.0, 6.0, ((0, 96), (3, 8))),
        "error_buffer": centred(keys[1], (REPLICAS, 2, ROWS, FF), 0.5, 4.0, ((0, 96), (3, 8)), jnp.float32),
        "q_warm": centred(keys[2], (2, FF, RANK), FF ** -0.5, 0.046875, ((1, 8),), jnp.float32),
    }


def orthonormal(p_sum):
    gram = jnp.einsum('nr,ns->rs', p_sum, p_sum, precision=lax.Precision.HIGHEST)
    lower = jnp.linalg.cholesky(gram)
    solved = jax.scipy.linalg.solve_triangular(lower, p_sum.T, lower=True)
    return solved.T

def reference(gradient, error_buffer, q_warm):

    def add_p(total, pair):
        corrected = pair[0].astype(jnp.float32) + pair[1]
        return (total + jnp.einsum('knf,kfr->knr', corrected, q_warm, precision=lax.Precision.HIGHEST), None)
    p_sum, _ = lax.scan(add_p, jnp.zeros((2, ROWS, RANK), jnp.float32), (gradient, error_buffer))
    p_factor = jax.vmap(orthonormal)(p_sum)

    def add_q(total, pair):
        corrected = pair[0].astype(jnp.float32) + pair[1]
        return (total + jnp.einsum('knf,knr->kfr', corrected, p_factor, precision=lax.Precision.HIGHEST), None)
    q_factor, _ = lax.scan(add_q, jnp.zeros((2, FF, RANK), jnp.float32), (gradient, error_buffer))
    decompressed = jnp.einsum('knr,kfr->knf', p_factor, q_factor, precision=lax.Precision.HIGHEST) / REPLICAS
    new_error = gradient.astype(jnp.float32) + error_buffer - decompressed[None]
    return (new_error, p_factor, q_factor)
```

```python
import functools

import jax
import jax.numpy as jnp
from jax import lax
from jax.experimental import pallas as pl
from jax.experimental.pallas import tpu as pltpu
from jax.sharding import PartitionSpec as P

HI = lax.Precision.HIGHEST
NX, NZ, NYL = 4, 12, 4
NY = 2 * NYL
FD = 1792
UNITS = 56
CH = 5
QU = NZ * CH
FAR_FIRST = (6, 5, 7, 4, 8, 3, 9, 2, 10, 1, 11, 0)
NEAR_FIRST = (1, 11, 2, 10, 3, 9, 4, 8, 5, 7, 6)
NT = (((1,), (1,)), ((), ()))


def dot(a, b):
    return jnp.dot(a, b, precision=HI, preferred_element_type=jnp.float32)


def dot_nt(a, b):
    return lax.dot_general(a, b, NT, precision=HI, preferred_element_type=jnp.float32)


def halves(a):
    hi = a.astype(jnp.bfloat16)
    return hi, (a - hi.astype(jnp.float32)).astype(jnp.bfloat16)


def dot3(a, b):
    (ah, al), (bh, bl) = a, halves(b)
    f = functools.partial(jnp.dot, preferred_element_type=jnp.float32)
    return f(ah, bh) + (f(ah, bl) + f(al, bh))


def inverse_factors(grams):
    rows = lax.broadcasted_iota(jnp.int32, (8, 128), 0)
    lanes = lax.broadcasted_iota(jnp.int32, (8, 128), 1)
    ms = []
    for g in grams:
        blocks = []
        for b in range(8):
            eye = jnp.where(lanes[:, :64] == rows[:, :64] + 8 * b, 1.0, 0.0)
            blocks.append(jnp.concatenate([g[8 * b : 8 * b + 8], eye.astype(jnp.float32)], axis=1))
        ms.append(blocks)
    for j in range(63):
        jb, ji = divmod(j, 8)
        for m in ms:
            row = m[jb][ji : ji + 1]
            scaled = row / row[:, j : j + 1]
            for b in range(jb, 8):
                col = m[b][:, j : j + 1]
                if b == jb:
                    col = jnp.where(rows[:, :1] > ji, col, 0.0)
                m[b] = m[b] - col * scaled
    out = []
    for m in ms:
        parts = []
        for b in range(8):
            d = jnp.sum(jnp.where(lanes == rows + 8 * b, m[b], 0.0), axis=1, keepdims=True)
            parts.append(m[b][:, 64:] / jnp.sqrt(d))
        out.append(jnp.concatenate(parts, axis=0))
    return out


def kernel(
    g_ref, e_ref, w_ref, err_ref, p_ref, q_ref,
    st, xr, zs, zr, ys, yr, p1s, p1r, p2, p3, pf, qf,
    s1, r1, s2, r2, s3, r3, s4, r4, sx, rx, sz, rz, sy, ry, saz, raz, sax, rax,
):
    dp, tensor = lax.axis_index("dp"), lax.axis_index("tensor")
    z = lax.rem(dp, NZ)
    xa = lax.div(dp, NZ)
    x = lax.rem(xa, NX)
    yh = lax.div(xa, NX)
    yl, core = lax.div(tensor, 2), lax.rem(tensor, 2)
    y = yh * NYL + yl

    def at(yy, xx, zz, cc):
        return {"dp": (lax.div(yy, NYL) * NX + xx) * NZ + zz, "tensor": lax.rem(yy, NYL) * 2 + cc}

    def x_of(d):
        return lax.rem(x + d, NX)

    def z_of(d):
        return lax.rem(z + d, NZ)

    def y_of(d):
        return lax.rem(y + d, NY)

    def xc_peer(s):
        return at(y, x_of(s // 2), z, 1 - core if s % 2 else core)

    def x_peer(d):
        return at(y, x_of(d), z, core)

    def z_peer(d):
        return at(y, x, z_of(d), core)

    def y_peer(d):
        return at(y_of(d), x, z, core)

    def copy(src, dst, send, recv, to):
        c = pltpu.make_async_remote_copy(
            src_ref=src, dst_ref=dst, send_sem=send, recv_sem=recv, device_id=to, device_id_type=pl.DeviceIdType.MESH
        )
        c.start()
        return c

    barrier = pltpu.get_barrier_semaphore()
    peers = [xc_peer(s) for s in range(1, 8)] + [y_peer(d) for d in range(1, NY)] + [z_peer(d) for d in range(1, NZ)]
    for peer in peers:
        pl.semaphore_signal(barrier, inc=1, device_id=peer, device_id_type=pl.DeviceIdType.MESH)

    for xq in range(NX):
        st[xq * QU + UNITS : (xq + 1) * QU] = jnp.zeros((QU - UNITS, 8, 256), jnp.float32)
    for j in range(FD // 128):
        cols = slice(128 * j, 128 * j + 128)
        c = g_ref[:, cols].astype(jnp.float32) + e_ref[:, cols]
        err_ref[:, cols] = c
        t = c.T.reshape(16, 8, 256)
        for h in (2 * j, 2 * j + 1):
            base = (h // 7) * QU + (h % 7) * 8
            st[base : base + 8] = t[(h - 2 * j) * 8 : (h - 2 * j) * 8 + 8]
    for k in range(2):
        part = dot_nt(w_ref[64 * k : 64 * k + 64], err_ref[128 * k : 128 * k + 128])
        p1s[4 * k : 4 * k + 4] = part.reshape(4, 16, 128)

    pl.semaphore_wait(barrier, len(peers))

    owner = x * 2 + core
    c1 = []
    for s in range(1, 8):
        to = x_of(s // 2) * 2 + (1 - core if s % 2 else core)
        c1.append(copy(p1s.at[to], p1r.at[s], s1.at[s], r1.at[s], xc_peer(s)))

    cx = {}
    for i, off in enumerate(FAR_FIRST):
        zt = z_of(off)
        for d in (2, 1, 3):
            cx[d, off] = copy(
                st.at[pl.ds(x_of(d) * QU + zt * CH, CH)],
                xr.at[d - 1, pl.ds(off * CH, CH)],
                sx.at[d - 1, off], rx.at[d - 1, off], x_peer(d),
            )

    for c in c1:
        c.wait_recv()
    total = p1s[pl.ds(owner, 1)]
    for s in range(1, 8):
        total = total + p1r[s : s + 1]
    p2[pl.ds(y, 1)] = total
    c2 = [copy(p2.at[y], p2.at[y], s2.at[d], r2.at[d], y_peer(d)) for d in (4, 3, 5, 2, 6, 1, 7)]

    cz = {}

    def forward(off):
        for d in (1, 3, 2):
            cx[d, off].wait_recv()
        own = st[pl.ds(x * QU + z_of(off) * CH, CH)]
        here = slice(off * CH, off * CH + CH)
        zs[here] = (own + xr[0, here]) + (xr[1, here] + xr[2, here])
        if off:
            cz[off] = copy(zs.at[pl.ds(off * CH, CH)], zr.at[off], sz.at[off], rz.at[off], z_peer(off))

    for off in FAR_FIRST[:3]:
        forward(off)

    for c in c2:
        c.wait_recv()
    total = p2[0:1]
    for i in range(1, NY):
        total = total + p2[i : i + 1]
    p3[pl.ds(z, 1)] = total
    c3 = [copy(p3.at[z], p3.at[z], s3.at[d], r3.at[d], z_peer(d)) for d in FAR_FIRST[:-1]]

    for off in FAR_FIRST[3:8]:
        forward(off)

    for c in c3:
        c.wait_recv()
    total = p3[0:1]
    for i in range(1, NZ):
        total = total + p3[i : i + 1]
    pf[pl.ds(owner, 1)] = total
    c4 = [copy(pf.at[owner], pf.at[owner], s4.at[s], r4.at[s], xc_peer(s)) for s in range(1, 8)]

    for off in FAR_FIRST[8:]:
        forward(off)

    for c in c4:
        c.wait_recv()
    pt = pf[...].reshape(128, 128)
    pk = [pt[:64], pt[64:]]
    inv = inverse_factors([dot_nt(a, a) for a in pk])
    factor = jnp.concatenate([dot(inv[k], pk[k]) for k in range(2)], axis=0)
    p_ref[...] = factor
    flipped = factor.T
    lane = lax.broadcasted_iota(jnp.int32, (128, 128), 1)
    p_wide = jnp.concatenate([jnp.where(lane < 64, flipped, 0.0), jnp.where(lane < 64, 0.0, flipped)], axis=0)

    for off in FAR_FIRST[:-1]:
        cz[off].wait_recv()
    total = zs[0:CH]
    for off in range(1, NZ):
        total = total + zr[off]
    ys[...] = total
    cy = copy(ys, yr, sy, ry, y_peer(NYL))
    cy.wait_recv()
    summed = ys[...] + yr[...]

    mine = pl.ds(x * QU + z * CH, CH)
    qf[mine] = dot(summed.reshape(CH * 8, 256), p_wide).reshape(CH, 8, 128)
    caz = {off: copy(qf.at[mine], qf.at[mine], saz.at[off], raz.at[off], z_peer(off)) for off in FAR_FIRST[:-1]}
    cax = []

    def spread(off):
        piece = pl.ds(x * QU + z_of(NZ - off) * CH, CH)
        for d in (2, 1, 3):
            cax.append(copy(qf.at[piece], qf.at[piece], sax.at[d - 1, off], rax.at[d - 1, off], x_peer(d)))

    spread(0)
    for off in NEAR_FIRST:
        caz[off].wait_recv()
        spread(off)
    for c in cax:
        c.wait_recv()

    p_parts = halves(p_wide * (1.0 / (2 * NX * NZ)))
    for j in range(FD // 128):
        cols = slice(128 * j, 128 * j + 128)
        rows = []
        for h in (2 * j, 2 * j + 1):
            base = (h // 7) * QU + (h % 7) * 8
            rows.append(qf[base : base + 8].reshape(64, 128))
        qt = jnp.concatenate(rows, axis=0).T
        q_ref[:, cols] = qt
        err_ref[:, cols] = err_ref[:, cols] - dot3(p_parts, qt)

    for c in c1 + c2 + c3 + c4 + list(cx.values()) + list(cz.values()) + [cy] + list(caz.values()) + cax:
        c.wait_send()


def local(gradient, error_buffer, q_warm):
    g = gradient.reshape(256, FD)
    e = error_buffer.reshape(256, FD)
    w = jnp.swapaxes(q_warm, 1, 2).reshape(128, FD)
    f32 = jnp.float32
    dma = pltpu.SemaphoreType.DMA
    vmem = pl.BlockSpec(memory_space=pltpu.VMEM)
    err, pt, qt = pl.pallas_call(
        kernel,
        out_shape=(
            jax.ShapeDtypeStruct((256, FD), f32),
            jax.ShapeDtypeStruct((128, 128), f32),
            jax.ShapeDtypeStruct((128, FD), f32),
        ),
        in_specs=[vmem] * 3,
        out_specs=(vmem,) * 3,
        scratch_shapes=[
            pltpu.VMEM((NX * QU, 8, 256), f32),
            pltpu.VMEM((3, QU, 8, 256), f32),
            pltpu.VMEM((QU, 8, 256), f32),
            pltpu.VMEM((NZ, CH, 8, 256), f32),
            pltpu.VMEM((CH, 8, 256), f32),
            pltpu.VMEM((CH, 8, 256), f32),
            pltpu.VMEM((8, 16, 128), f32),
            pltpu.VMEM((8, 16, 128), f32),
            pltpu.VMEM((NY, 16, 128), f32),
            pltpu.VMEM((NZ, 16, 128), f32),
            pltpu.VMEM((8, 16, 128), f32),
            pltpu.VMEM((NX * QU, 8, 128), f32),
            dma((8,)), dma((8,)), dma((8,)), dma((8,)), dma((12,)), dma((12,)), dma((8,)), dma((8,)),
            dma((3, 12)), dma((3, 12)), dma((12,)), dma((12,)), dma, dma,
            dma((12,)), dma((12,)), dma((3, 12)), dma((3, 12)),
        ],
        compiler_params=pltpu.CompilerParams(
            collective_id=0, has_side_effects=True, vmem_limit_bytes=48 * 1024 * 1024
        ),
    )(g, e, w)
    p_factor = jnp.swapaxes(pt.reshape(2, 64, 128), 1, 2)
    q_factor = jnp.swapaxes(qt.reshape(2, 64, FD), 1, 2)
    return err.reshape(1, 2, 128, FD), p_factor, q_factor


def solution(mesh):
    in_specs = (
        P("dp", None, None, "tensor"),
        P("dp", None, None, "tensor"),
        P(None, "tensor", None),
    )
    out_specs = (P("dp", None, None, "tensor"), P(), P(None, "tensor", None))
    return jax.shard_map(local, mesh=mesh, in_specs=in_specs, out_specs=out_specs, check_vma=False)
```

```python
import functools

import jax
import jax.numpy as jnp
from jax import lax
from jax.experimental import pallas as pl
from jax.experimental.pallas import tpu as pltpu
from jax.sharding import PartitionSpec as P

HI = lax.Precision.HIGHEST
NX, NZ, NYL = 4, 12, 4
NY = 2 * NYL
FD = 1792
UNITS = 56
CH = 5
QU = NZ * CH
FAR_FIRST = (6, 5, 7, 4, 8, 3, 9, 2, 10, 1, 11, 0)
NEAR_FIRST = (1, 11, 2, 10, 3, 9, 4, 8, 5, 7, 6)
NT = (((1,), (1,)), ((), ()))


def dot(a, b):
    return jnp.dot(a, b, precision=HI, preferred_element_type=jnp.float32)


def dot_nt(a, b):
    return lax.dot_general(a, b, NT, precision=HI, preferred_element_type=jnp.float32)


def halves(a):
    hi = a.astype(jnp.bfloat16)
    return hi, (a - hi.astype(jnp.float32)).astype(jnp.bfloat16)


def dot3(a, b):
    (ah, al), (bh, bl) = a, halves(b)
    f = functools.partial(jnp.dot, preferred_element_type=jnp.float32)
    return f(ah, bh) + (f(ah, bl) + f(al, bh))


def index_of(axis):
    return lax.broadcasted_iota(jnp.int32, (8, 128), axis)


def augmented(g):
    blocks = []
    for b in range(8):
        eye = jnp.where(index_of(1)[:, :64] == index_of(0)[:, :64] + 8 * b, 1.0, 0.0)
        blocks.append(jnp.concatenate([g[8 * b : 8 * b + 8], eye], axis=1))
    return blocks


def eliminate(ms):
    for jb in range(8):
        spread = [
            [[jnp.broadcast_to(m[b][:, j : j + 1], (8, 128)) for b in range(jb, 8)] for j in range(8 * jb, 8 * jb + 8)]
            for m in ms
        ]
        for ji in range(8):
            for m, columns in zip(ms, spread):
                column = columns[ji]
                pivot = 1.0 / column[0][ji : ji + 1]
                below = [jnp.where(index_of(0) > ji, column[0], 0.0)] + column[1:]
                for jj in range(ji + 1, 8):
                    factor = column[0][jj : jj + 1] * pivot
                    columns[jj] = [a - b * factor for a, b in zip(columns[jj], below)]
                row = m[jb][ji : ji + 1] * pivot
                for b in range(jb, 8):
                    m[b] = m[b] - below[b - jb] * row


def inverse_factor(m):
    parts = []
    for b in range(8):
        d = jnp.sum(jnp.where(index_of(1) == index_of(0) + 8 * b, m[b], 0.0), axis=1, keepdims=True)
        parts.append(m[b][:, 64:] / jnp.sqrt(d))
    return jnp.concatenate(parts, axis=0)


def kernel(
    c_ref, w_ref, p_ref, qf,
    st, xr, zs, zr, ys, yr, p1s, p1r, p2, p3, pf,
    s1, r1, sf, rf, s2, r2, s3, r3, s4, r4, sx, rx, sz, rz, sy, ry, saz, raz, sax, rax,
):
    dp, tensor = lax.axis_index("dp"), lax.axis_index("tensor")
    z = lax.rem(dp, NZ)
    xa = lax.div(dp, NZ)
    x = lax.rem(xa, NX)
    yh = lax.div(xa, NX)
    yl, core = lax.div(tensor, 2), lax.rem(tensor, 2)
    y = yh * NYL + yl

    def at(yy, xx, zz, cc):
        return {"dp": (lax.div(yy, NYL) * NX + xx) * NZ + zz, "tensor": lax.rem(yy, NYL) * 2 + cc}

    def x_of(d):
        return lax.rem(x + d, NX)

    def z_of(d):
        return lax.rem(z + d, NZ)

    def y_of(d):
        return lax.rem(y + d, NY)

    def xc_peer(s):
        return at(y, x_of(s // 2), z, 1 - core if s % 2 else core)

    def x_peer(d):
        return at(y, x_of(d), z, core)

    def z_peer(d):
        return at(y, x, z_of(d), core)

    def y_peer(d):
        return at(y_of(d), x, z, core)

    def copy(src, dst, send, recv, to):
        c = pltpu.make_async_remote_copy(
            src_ref=src, dst_ref=dst, send_sem=send, recv_sem=recv, device_id=to, device_id_type=pl.DeviceIdType.MESH
        )
        c.start()
        return c

    barrier = pltpu.get_barrier_semaphore()
    peers = [xc_peer(s) for s in range(1, 8)] + [y_peer(d) for d in range(1, NY)] + [z_peer(d) for d in range(1, NZ)]
    for peer in peers:
        pl.semaphore_signal(barrier, inc=1, device_id=peer, device_id_type=pl.DeviceIdType.MESH)

    for xq in range(NX):
        st[xq * QU + UNITS : (xq + 1) * QU] = jnp.zeros((QU - UNITS, 8, 256), jnp.float32)
    def runs(i):
        return [(h // 7) * QU + (h % 7) * 8 for h in range(4 * i, 4 * i + 4)]

    for i in range(FD // 256):
        t = c_ref[:, 256 * i : 256 * i + 256].T.reshape(32, 8, 256)
        for n, base in enumerate(runs(i)):
            st[base : base + 8] = t[8 * n : 8 * n + 8]

    pl.semaphore_wait(barrier, len(peers))

    cf, cx, cz = {}, {}, {}

    def cut(off):
        return 3 if FAR_FIRST.index(off) % 2 else 2

    def scatter(off):
        base, n = x_of(2) * QU + z_of(off) * CH, cut(off)
        cf[1, off] = copy(
            st.at[pl.ds(base, n)], xr.at[2, pl.ds(off * CH, n)], sf.at[0, off], rf.at[0, off], x_peer(1)
        )
        cf[3, off] = copy(
            st.at[pl.ds(base + n, CH - n)], xr.at[2, pl.ds(off * CH + n, CH - n)],
            sf.at[1, off], rf.at[1, off], x_peer(3),
        )

    def relay(off):
        n = cut(off)
        for d, lo, hi in ((1, 0, n), (3, n, CH)):
            base = x_of(d) * QU + z_of(off) * CH
            cf[d, off].wait_recv()
            there = pl.ds(base + lo, hi - lo)
            st[there] = st[there] + xr[2, off * CH + lo : off * CH + hi]
            cx[d, off] = copy(
                st.at[pl.ds(base, CH)], xr.at[d // 2, pl.ds(off * CH, CH)],
                sx.at[d // 2, off], rx.at[d // 2, off], x_peer(d),
            )

    def forward(off):
        for d in (1, 3):
            cx[d, off].wait_recv()
        own = st[pl.ds(x * QU + z_of(off) * CH, CH)]
        here = slice(off * CH, off * CH + CH)
        zs[here] = own + (xr[0, here] + xr[1, here])
        if off:
            cz[off] = copy(zs.at[pl.ds(off * CH, CH)], zr.at[off], sz.at[off], rz.at[off], z_peer(off))

    for off in FAR_FIRST[:2]:
        scatter(off)

    parts = [jnp.zeros((64, 128), jnp.float32)] * 2
    for i in range(FD // 256):
        t = jnp.concatenate([st[base : base + 8].reshape(64, 256) for base in runs(i)], axis=0)
        w = halves(w_ref[:, 256 * i : 256 * i + 256])
        for k in range(2):
            wk = [a[64 * k : 64 * k + 64] for a in w]
            parts[k] = parts[k] + dot3(wk, t[:, 128 * k : 128 * k + 128])
    for k in range(2):
        p1s[4 * k : 4 * k + 4] = parts[k].reshape(4, 16, 128)

    owner = x * 2 + core
    c1 = []
    for s in range(1, 8):
        to = x_of(s // 2) * 2 + (1 - core if s % 2 else core)
        c1.append(copy(p1s.at[to], p1r.at[s], s1.at[s], r1.at[s], xc_peer(s)))

    for off in FAR_FIRST[2:]:
        scatter(off)

    for c in c1:
        c.wait_recv()
    total = p1s[pl.ds(owner, 1)]
    for s in range(1, 8):
        total = total + p1r[s : s + 1]
    p3[pl.ds(z, 1)] = total
    c3 = [copy(p3.at[z], p3.at[z], s3.at[d], r3.at[d], z_peer(d)) for d in FAR_FIRST[:-1]]

    for off in FAR_FIRST[:3]:
        relay(off)
    for i in range(3, 7):
        relay(FAR_FIRST[i])
        forward(FAR_FIRST[i - 3])

    for c in c3:
        c.wait_recv()
    total = p3[0:1]
    for i in range(1, NZ):
        total = total + p3[i : i + 1]
    p2[pl.ds(y, 1)] = total
    c2 = [copy(p2.at[y], p2.at[y], s2.at[d], r2.at[d], y_peer(d)) for d in (4, 3, 5, 2, 6, 1, 7)]

    for i in range(7, 12):
        if i < NZ:
            relay(FAR_FIRST[i])
        forward(FAR_FIRST[i - 3])

    for c in c2:
        c.wait_recv()
    total = p2[0:1]
    for i in range(1, NY):
        total = total + p2[i : i + 1]
    pf[pl.ds(owner, 1)] = total
    c4 = [copy(pf.at[owner], pf.at[owner], s4.at[s], r4.at[s], xc_peer(s)) for s in range(1, 8)]

    for off in FAR_FIRST[9:]:
        forward(off)

    total = zs[0:CH]
    for off in FAR_FIRST[:-1]:
        cz[off].wait_recv()
        total = total + zr[off]
    ys[...] = total
    cy = copy(ys, yr, sy, ry, y_peer(NYL))

    for c in c4:
        c.wait_recv()
    pt = pf[...].reshape(128, 128)
    pk = [pt[:64], pt[64:]]
    ms = [augmented(dot_nt(a, a)) for a in pk]
    eliminate(ms)
    inv = [inverse_factor(m) for m in ms]
    factor = jnp.concatenate([dot(inv[k], pk[k]) for k in range(2)], axis=0)
    p_ref[...] = factor
    flipped = factor.T
    lane = lax.broadcasted_iota(jnp.int32, (128, 128), 1)
    p_wide = jnp.concatenate([jnp.where(lane < 64, flipped, 0.0), jnp.where(lane < 64, 0.0, flipped)], axis=0)

    cy.wait_recv()
    summed = ys[...] + yr[...]

    mine = pl.ds(x * QU + z * CH, CH)
    qf[mine] = dot(summed.reshape(CH * 8, 256), p_wide).reshape(CH, 8, 128)
    caz = {off: copy(qf.at[mine], qf.at[mine], saz.at[off], raz.at[off], z_peer(off)) for off in NEAR_FIRST}
    cax = []

    def spread(off):
        piece = pl.ds(x * QU + z_of(NZ - off) * CH, CH)
        for d in (2, 1, 3):
            cax.append(copy(qf.at[piece], qf.at[piece], sax.at[d - 1, off], rax.at[d - 1, off], x_peer(d)))

    spread(0)
    for off in NEAR_FIRST:
        caz[off].wait_recv()
        spread(off)
    for c in cax:
        c.wait_recv()

    for c in c1 + c2 + c3 + c4 + list(cf.values()) + list(cx.values()) + list(cz.values()) + [cy] + list(caz.values()) + cax:
        c.wait_send()


def last(c_ref, p_ref, qf, err_hbm, p_hbm, q_hbm, err, q, se, sp, sq):
    stores = [pltpu.make_async_copy(p_ref, p_hbm, sp)]
    stores[0].start()
    flipped = p_ref[...].T * (1.0 / (2 * NX * NZ))
    lane = lax.broadcasted_iota(jnp.int32, (128, 128), 1)
    wide = jnp.concatenate([jnp.where(lane < 64, flipped, 0.0), jnp.where(lane < 64, 0.0, flipped)], axis=0)
    p_parts = halves(wide)
    for i in range(FD // 256):
        cols = slice(256 * i, 256 * i + 256)
        rows = [(h // 7) * QU + (h % 7) * 8 for h in range(4 * i, 4 * i + 4)]
        qt = jnp.concatenate([qf[base : base + 8].reshape(64, 128) for base in rows], axis=0).T
        q[:, cols] = qt
        err[:, cols] = c_ref[:, cols] - dot3(p_parts, qt)
        there = pl.ds(256 * i, 256)
        stores.append(pltpu.make_async_copy(err.at[:, there], err_hbm.at[:, there], se.at[i]))
        stores.append(pltpu.make_async_copy(q.at[:, there], q_hbm.at[:, there], sq.at[i]))
        for c in stores[-2:]:
            c.start()
    for c in stores:
        c.wait()


def local(gradient, error_buffer, q_warm):
    c = (gradient.astype(jnp.float32) + error_buffer).reshape(256, FD)
    w = jnp.swapaxes(q_warm, 1, 2).reshape(128, FD)
    f32 = jnp.float32
    dma = pltpu.SemaphoreType.DMA
    vmem = pl.BlockSpec(memory_space=pltpu.VMEM)
    hbm = pl.BlockSpec(memory_space=pltpu.HBM)
    pt, qf = pl.pallas_call(
        kernel,
        out_shape=(
            jax.ShapeDtypeStruct((128, 128), f32),
            jax.ShapeDtypeStruct((NX * QU, 8, 128), f32),
        ),
        in_specs=[vmem] * 2,
        out_specs=(vmem,) * 2,
        scratch_shapes=[
            pltpu.VMEM((NX * QU, 8, 256), f32),
            pltpu.VMEM((3, QU, 8, 256), f32),
            pltpu.VMEM((QU, 8, 256), f32),
            pltpu.VMEM((NZ, CH, 8, 256), f32),
            pltpu.VMEM((CH, 8, 256), f32),
            pltpu.VMEM((CH, 8, 256), f32),
            pltpu.VMEM((8, 16, 128), f32),
            pltpu.VMEM((8, 16, 128), f32),
            pltpu.VMEM((NY, 16, 128), f32),
            pltpu.VMEM((NZ, 16, 128), f32),
            pltpu.VMEM((8, 16, 128), f32),
            dma((8,)), dma((8,)), dma((2, 12)), dma((2, 12)), dma((8,)), dma((8,)), dma((12,)), dma((12,)), dma((8,)), dma((8,)),
            dma((2, 12)), dma((2, 12)), dma((12,)), dma((12,)), dma, dma,
            dma((12,)), dma((12,)), dma((3, 12)), dma((3, 12)),
        ],
        compiler_params=pltpu.CompilerParams(
            collective_id=0, has_side_effects=True, vmem_limit_bytes=24 * 1024 * 1024
        ),
    )(c, w)
    err, pt, qt = pl.pallas_call(
        last,
        out_shape=(
            jax.ShapeDtypeStruct((256, FD), f32),
            jax.ShapeDtypeStruct((128, 128), f32),
            jax.ShapeDtypeStruct((128, FD), f32),
        ),
        in_specs=[vmem] * 3,
        out_specs=(hbm,) * 3,
        scratch_shapes=[pltpu.VMEM((256, FD), f32), pltpu.VMEM((128, FD), f32), dma((7,)), dma, dma((7,))],
        compiler_params=pltpu.CompilerParams(vmem_limit_bytes=16 * 1024 * 1024),
    )(c, pt, qf)
    p_factor = jnp.swapaxes(pt.reshape(2, 64, 128), 1, 2)
    q_factor = jnp.swapaxes(qt.reshape(2, 64, FD), 1, 2)
    return err.reshape(1, 2, 128, FD), p_factor, q_factor


def solution(mesh):
    in_specs = (
        P("dp", None, None, "tensor"),
        P("dp", None, None, "tensor"),
        P(None, "tensor", None),
    )
    out_specs = (P("dp", None, None, "tensor"), P(), P(None, "tensor", None))
    return jax.shard_map(local, mesh=mesh, in_specs=in_specs, out_specs=out_specs, check_vma=False)
```

```python
import functools

import jax
import jax.numpy as jnp
from jax import lax
from jax.experimental import pallas as pl
from jax.experimental.pallas import tpu as pltpu
from jax.sharding import PartitionSpec as P

HI = lax.Precision.HIGHEST
NX, NZ, NYL = 4, 12, 4
NY = 2 * NYL
FD = 1792
UNITS = 56
CH = 5
QU = NZ * CH
HALF = 2
FAR_FIRST = (6, 5, 7, 4, 8, 3, 9, 2, 10, 1, 11, 0)
NEAR_FIRST = (1, 11, 2, 10, 3, 9, 4, 8, 5, 7, 6)
NT = (((1,), (1,)), ((), ()))


def dot(a, b):
    return jnp.dot(a, b, precision=HI, preferred_element_type=jnp.float32)


def dot_nt(a, b):
    return lax.dot_general(a, b, NT, precision=HI, preferred_element_type=jnp.float32)


def halves(a):
    hi = a.astype(jnp.bfloat16)
    return hi, (a - hi.astype(jnp.float32)).astype(jnp.bfloat16)


def dot3(a, b):
    (ah, al), (bh, bl) = a, halves(b)
    f = functools.partial(jnp.dot, preferred_element_type=jnp.float32)
    return f(ah, bh) + (f(ah, bl) + f(al, bh))


def index_of(axis):
    return lax.broadcasted_iota(jnp.int32, (8, 128), axis)


def augmented(g):
    blocks = []
    for b in range(8):
        eye = jnp.where(index_of(1)[:, :64] == index_of(0)[:, :64] + 8 * b, 1.0, 0.0)
        blocks.append(jnp.concatenate([g[8 * b : 8 * b + 8], eye], axis=1))
    return blocks


def eliminate(ms):
    for jb in range(8):
        spread = [
            [[jnp.broadcast_to(m[b][:, j : j + 1], (8, 128)) for b in range(jb, 8)] for j in range(8 * jb, 8 * jb + 8)]
            for m in ms
        ]
        for ji in range(8):
            for m, columns in zip(ms, spread):
                column = columns[ji]
                pivot = 1.0 / column[0][ji : ji + 1]
                below = [jnp.where(index_of(0) > ji, column[0], 0.0)] + column[1:]
                for jj in range(ji + 1, 8):
                    factor = column[0][jj : jj + 1] * pivot
                    columns[jj] = [a - b * factor for a, b in zip(columns[jj], below)]
                row = m[jb][ji : ji + 1] * pivot
                for b in range(jb, 8):
                    m[b] = m[b] - below[b - jb] * row


def inverse_factor(m):
    parts = []
    for b in range(8):
        d = jnp.sum(jnp.where(index_of(1) == index_of(0) + 8 * b, m[b], 0.0), axis=1, keepdims=True)
        parts.append(m[b][:, 64:] / jnp.sqrt(d))
    return jnp.concatenate(parts, axis=0)


def kernel(
    c_ref, w_ref, p_ref, qf,
    st, xr, zs, zr, ys, yr, p1s, p1r, p2, p3, pf,
    s1, r1, sf, rf, s2, r2, s3, r3, s4, r4, sx, rx, sz, rz, sy, ry, saz, raz, sax, rax,
):
    dp, tensor = lax.axis_index("dp"), lax.axis_index("tensor")
    z = lax.rem(dp, NZ)
    xa = lax.div(dp, NZ)
    x = lax.rem(xa, NX)
    yh = lax.div(xa, NX)
    yl, core = lax.div(tensor, 2), lax.rem(tensor, 2)
    y = yh * NYL + yl

    def at(yy, xx, zz, cc):
        return {"dp": (lax.div(yy, NYL) * NX + xx) * NZ + zz, "tensor": lax.rem(yy, NYL) * 2 + cc}

    def x_of(d):
        return lax.rem(x + d, NX)

    def z_of(d):
        return lax.rem(z + d, NZ)

    def y_of(d):
        return lax.rem(y + d, NY)

    def xc_peer(s):
        return at(y, x_of(s // 2), z, 1 - core if s % 2 else core)

    def x_peer(d):
        return at(y, x_of(d), z, core)

    def z_peer(d):
        return at(y, x, z_of(d), core)

    def y_peer(d):
        return at(y_of(d), x, z, core)

    def copy(src, dst, send, recv, to):
        c = pltpu.make_async_remote_copy(
            src_ref=src, dst_ref=dst, send_sem=send, recv_sem=recv, device_id=to, device_id_type=pl.DeviceIdType.MESH
        )
        c.start()
        return c

    barrier = pltpu.get_barrier_semaphore()
    peers = [xc_peer(s) for s in range(1, 8)] + [y_peer(d) for d in range(1, NY)] + [z_peer(d) for d in range(1, NZ)]
    for peer in peers:
        pl.semaphore_signal(barrier, inc=1, device_id=peer, device_id_type=pl.DeviceIdType.MESH)

    for xq in range(NX):
        st[xq * QU + UNITS : (xq + 1) * QU] = jnp.zeros((QU - UNITS, 8, 256), jnp.float32)
    def runs(i):
        return [(h // 7) * QU + (h % 7) * 8 for h in range(4 * i, 4 * i + 4)]

    for i in range(FD // 256):
        t = c_ref[:, 256 * i : 256 * i + 256].T.reshape(32, 8, 256)
        for n, base in enumerate(runs(i)):
            st[base : base + 8] = t[8 * n : 8 * n + 8]

    pl.semaphore_wait(barrier, len(peers))

    cf, cx, cz = {}, {}, {}

    def cut(off):
        return 3 if FAR_FIRST.index(off) % 2 else 2

    def scatter(off):
        base, n = x_of(2) * QU + z_of(off) * CH, cut(off)
        cf[1, off] = copy(
            st.at[pl.ds(base, n)], xr.at[2, pl.ds(off * CH, n)], sf.at[0, off], rf.at[0, off], x_peer(1)
        )
        cf[3, off] = copy(
            st.at[pl.ds(base + n, CH - n)], xr.at[2, pl.ds(off * CH + n, CH - n)],
            sf.at[1, off], rf.at[1, off], x_peer(3),
        )

    def relay(off):
        n = cut(off)
        for d, lo, hi in ((1, 0, n), (3, n, CH)):
            base = x_of(d) * QU + z_of(off) * CH
            cf[d, off].wait_recv()
            there = pl.ds(base + lo, hi - lo)
            st[there] = st[there] + xr[2, off * CH + lo : off * CH + hi]
            cx[d, off] = copy(
                st.at[pl.ds(base, CH)], xr.at[d // 2, pl.ds(off * CH, CH)],
                sx.at[d // 2, off], rx.at[d // 2, off], x_peer(d),
            )

    def forward(off):
        for d in (1, 3):
            cx[d, off].wait_recv()
        own = st[pl.ds(x * QU + z_of(off) * CH, CH)]
        here = slice(off * CH, off * CH + CH)
        total = own + (xr[0, here] + xr[1, here])
        if off in (1, 2, 10, 11):
            far = off + 3 if off < 6 else off - 3
            cz[far].wait_recv()
            total = total + zr[far]
        zs[here] = total
        if off in (3, 9):
            lo, hi = (0, HALF) if off == 3 else (HALF, CH)
            cz[6, off].wait_recv()
            part = slice(off * CH + lo, off * CH + hi)
            zs[part] = zs[part] + zr[6, lo:hi]
        if off == 6:
            for d, lo, hi, k in ((3, 0, HALF, 6), (9, HALF, CH, 0)):
                src, dst = zs.at[pl.ds(off * CH + lo, hi - lo)], zr.at[6, pl.ds(lo, hi - lo)]
                cz[6, d] = copy(src, dst, sz.at[k], rz.at[k], z_peer(d))
        elif off:
            to = 3 if off in (4, 5) else 9 if off in (7, 8) else off
            cz[off] = copy(zs.at[pl.ds(off * CH, CH)], zr.at[off], sz.at[off], rz.at[off], z_peer(to))

    for off in FAR_FIRST[:2]:
        scatter(off)

    parts = [jnp.zeros((64, 128), jnp.float32)] * 2
    for i in range(FD // 256):
        t = jnp.concatenate([st[base : base + 8].reshape(64, 256) for base in runs(i)], axis=0)
        w = halves(w_ref[:, 256 * i : 256 * i + 256])
        for k in range(2):
            wk = [a[64 * k : 64 * k + 64] for a in w]
            parts[k] = parts[k] + dot3(wk, t[:, 128 * k : 128 * k + 128])
    for k in range(2):
        p1s[4 * k : 4 * k + 4] = parts[k].reshape(4, 16, 128)

    owner = x * 2 + core
    c1 = []
    for s in range(1, 8):
        to = x_of(s // 2) * 2 + (1 - core if s % 2 else core)
        c1.append(copy(p1s.at[to], p1r.at[s], s1.at[s], r1.at[s], xc_peer(s)))

    for off in FAR_FIRST[2:]:
        scatter(off)

    for c in c1:
        c.wait_recv()
    total = p1s[pl.ds(owner, 1)]
    for s in range(1, 8):
        total = total + p1r[s : s + 1]
    p3[pl.ds(z, 1)] = total
    c3 = [copy(p3.at[z], p3.at[z], s3.at[d], r3.at[d], z_peer(d)) for d in FAR_FIRST[:-1]]

    for off in FAR_FIRST[:3]:
        relay(off)
    for i in range(3, 7):
        relay(FAR_FIRST[i])
        forward(FAR_FIRST[i - 3])

    for c in c3:
        c.wait_recv()
    total = p3[0:1]
    for i in range(1, NZ):
        total = total + p3[i : i + 1]
    p2[pl.ds(y, 1)] = total
    c2 = [copy(p2.at[y], p2.at[y], s2.at[d], r2.at[d], y_peer(d)) for d in (4, 3, 5, 2, 6, 1, 7)]

    for i in range(7, 12):
        if i < NZ:
            relay(FAR_FIRST[i])
        forward(FAR_FIRST[i - 3])

    for c in c2:
        c.wait_recv()
    total = p2[0:1]
    for i in range(1, NY):
        total = total + p2[i : i + 1]
    pf[pl.ds(owner, 1)] = total
    c4 = [copy(pf.at[owner], pf.at[owner], s4.at[s], r4.at[s], xc_peer(s)) for s in range(1, 8)]

    for off in FAR_FIRST[9:]:
        forward(off)

    total = zs[0:CH]
    for off in (3, 9, 2, 10, 1, 11):
        cz[off].wait_recv()
        total = total + zr[off]
    ys[...] = total
    cy = copy(ys, yr, sy, ry, y_peer(NYL))

    for c in c4:
        c.wait_recv()
    pt = pf[...].reshape(128, 128)
    pk = [pt[:64], pt[64:]]
    ms = [augmented(dot_nt(a, a)) for a in pk]
    eliminate(ms)
    inv = [inverse_factor(m) for m in ms]
    factor = jnp.concatenate([dot(inv[k], pk[k]) for k in range(2)], axis=0)
    p_ref[...] = factor
    flipped = factor.T
    lane = lax.broadcasted_iota(jnp.int32, (128, 128), 1)
    p_wide = jnp.concatenate([jnp.where(lane < 64, flipped, 0.0), jnp.where(lane < 64, 0.0, flipped)], axis=0)

    cy.wait_recv()
    summed = ys[...] + yr[...]

    mine = pl.ds(x * QU + z * CH, CH)
    qf[mine] = dot(summed.reshape(CH * 8, 256), p_wide).reshape(CH, 8, 128)
    caz = {off: copy(qf.at[mine], qf.at[mine], saz.at[off], raz.at[off], z_peer(off)) for off in NEAR_FIRST}
    cax = []

    def spread(off):
        piece = pl.ds(x * QU + z_of(NZ - off) * CH, CH)
        for d in (2, 1, 3):
            cax.append(copy(qf.at[piece], qf.at[piece], sax.at[d - 1, off], rax.at[d - 1, off], x_peer(d)))

    spread(0)
    for off in NEAR_FIRST:
        caz[off].wait_recv()
        spread(off)
    for c in cax:
        c.wait_recv()

    for c in c1 + c2 + c3 + c4 + list(cf.values()) + list(cx.values()) + list(cz.values()) + [cy] + list(caz.values()) + cax:
        c.wait_send()


def last(c_ref, p_ref, qf, err_hbm, p_hbm, q_hbm, err, q, se, sp, sq):
    stores = [pltpu.make_async_copy(p_ref, p_hbm, sp)]
    stores[0].start()
    flipped = p_ref[...].T * (1.0 / (2 * NX * NZ))
    lane = lax.broadcasted_iota(jnp.int32, (128, 128), 1)
    wide = jnp.concatenate([jnp.where(lane < 64, flipped, 0.0), jnp.where(lane < 64, 0.0, flipped)], axis=0)
    p_parts = halves(wide)
    for i in range(FD // 256):
        cols = slice(256 * i, 256 * i + 256)
        rows = [(h // 7) * QU + (h % 7) * 8 for h in range(4 * i, 4 * i + 4)]
        qt = jnp.concatenate([qf[base : base + 8].reshape(64, 128) for base in rows], axis=0).T
        q[:, cols] = qt
        err[:, cols] = c_ref[:, cols] - dot3(p_parts, qt)
        there = pl.ds(256 * i, 256)
        stores.append(pltpu.make_async_copy(err.at[:, there], err_hbm.at[:, there], se.at[i]))
        stores.append(pltpu.make_async_copy(q.at[:, there], q_hbm.at[:, there], sq.at[i]))
        for c in stores[-2:]:
            c.start()
    for c in stores:
        c.wait()


def local(gradient, error_buffer, q_warm):
    c = (gradient.astype(jnp.float32) + error_buffer).reshape(256, FD)
    w = jnp.swapaxes(q_warm, 1, 2).reshape(128, FD)
    f32 = jnp.float32
    dma = pltpu.SemaphoreType.DMA
    vmem = pl.BlockSpec(memory_space=pltpu.VMEM)
    hbm = pl.BlockSpec(memory_space=pltpu.HBM)
    pt, qf = pl.pallas_call(
        kernel,
        out_shape=(
            jax.ShapeDtypeStruct((128, 128), f32),
            jax.ShapeDtypeStruct((NX * QU, 8, 128), f32),
        ),
        in_specs=[vmem] * 2,
        out_specs=(vmem,) * 2,
        scratch_shapes=[
            pltpu.VMEM((NX * QU, 8, 256), f32),
            pltpu.VMEM((3, QU, 8, 256), f32),
            pltpu.VMEM((QU, 8, 256), f32),
            pltpu.VMEM((NZ, CH, 8, 256), f32),
            pltpu.VMEM((CH, 8, 256), f32),
            pltpu.VMEM((CH, 8, 256), f32),
            pltpu.VMEM((8, 16, 128), f32),
            pltpu.VMEM((8, 16, 128), f32),
            pltpu.VMEM((NY, 16, 128), f32),
            pltpu.VMEM((NZ, 16, 128), f32),
            pltpu.VMEM((8, 16, 128), f32),
            dma((8,)), dma((8,)), dma((2, 12)), dma((2, 12)), dma((8,)), dma((8,)), dma((12,)), dma((12,)), dma((8,)), dma((8,)),
            dma((2, 12)), dma((2, 12)), dma((12,)), dma((12,)), dma, dma,
            dma((12,)), dma((12,)), dma((3, 12)), dma((3, 12)),
        ],
        compiler_params=pltpu.CompilerParams(
            collective_id=0, has_side_effects=True, vmem_limit_bytes=24 * 1024 * 1024
        ),
    )(c, w)
    err, pt, qt = pl.pallas_call(
        last,
        out_shape=(
            jax.ShapeDtypeStruct((256, FD), f32),
            jax.ShapeDtypeStruct((128, 128), f32),
            jax.ShapeDtypeStruct((128, FD), f32),
        ),
        in_specs=[vmem] * 3,
        out_specs=(hbm,) * 3,
        scratch_shapes=[pltpu.VMEM((256, FD), f32), pltpu.VMEM((128, FD), f32), dma((7,)), dma, dma((7,))],
        compiler_params=pltpu.CompilerParams(vmem_limit_bytes=16 * 1024 * 1024),
    )(c, pt, qf)
    p_factor = jnp.swapaxes(pt.reshape(2, 64, 128), 1, 2)
    q_factor = jnp.swapaxes(qt.reshape(2, 64, FD), 1, 2)
    return err.reshape(1, 2, 128, FD), p_factor, q_factor


def solution(mesh):
    in_specs = (
        P("dp", None, None, "tensor"),
        P("dp", None, None, "tensor"),
        P(None, "tensor", None),
    )
    out_specs = (P("dp", None, None, "tensor"), P(), P(None, "tensor", None))
    return jax.shard_map(local, mesh=mesh, in_specs=in_specs, out_specs=out_specs, check_vma=False)
```
